256 devices in a mesh: rep: 4 (over x), ep: 64 (over y, z, core).
Axes of the slice: x: 4, y: 4, z: 8, core: 2. Of those that a mesh axis runs over, the one named last changes fastest.
Arguments:
- d_out: bfloat16 [32768, 2048], P(('rep', 'ep')), may hold values from -6 to 6
- saved_input: bfloat16 [32768, 2048], P(('rep', 'ep')), may hold values from -6 to 6
- routes: int32 [32768, 6], P(('rep', 'ep')), may hold values from 0 to 63, all different within a row; in each aligned block of 128 rows (0 to 127, 128 to 255, ...) at most 13 rows name the same one
- probs: bfloat16 [32768, 6], P(('rep', 'ep')), may hold values from 0.049804688 to 0.5
- gate_pre: bfloat16 [212992, 704], P(('rep', 'ep')), may hold values from -6 to 6
- up_pre: bfloat16 [212992, 704], P(('rep', 'ep')), may hold values from -6 to 6
- gate_weight: bfloat16 [64, 704, 2048], P('ep', 'rep'), may hold values from -0.125 to 0.125
- up_weight: bfloat16 [64, 704, 2048], P('ep', 'rep'), may hold values from -0.125 to 0.125
- down_weight: bfloat16 [64, 704, 2048], P('ep', 'rep'), may hold values from -0.21875 to 0.21875
Outputs:
- d_tokens: bfloat16 [32768, 2048], P(('rep', 'ep'))
- d_probs: bfloat16 [32768, 6], P(('rep', 'ep'))
- gate_weight_grad: float32 [64, 704, 2048], P('ep', 'rep')
- up_weight_grad: float32 [64, 704, 2048], P('ep', 'rep')
- down_weight_grad: float32 [64, 704, 2048], P('ep', 'rep')
The draws below stay inside these ranges and needn't reach their ends.
Inputs may be any that keep to these rules, and one draw needn't show every extreme that they name: `routes`: each row names 6 different experts. Among the 128 rows of one device no expert is named more than 13 times, and in some device's rows one expert is named exactly 13 times.
All inputs are finite; a program needn't handle non-finite values.
Results may differ from the reference program's by a relative error of at most 0.012.
Values may be sent and summed in bfloat16 or wider, within the bound.
A program may use at most 128 MiB of HBM per device.

```python
import math
import jax
import jax.numpy as jnp
import numpy as np
from jax import lax

D = 2048
H = 704
TOP = 6
T_DEV = 128
EXPERTS = 64
CAP = 13
SLOTS = 832
TOKENS = 32768
ALL_SLOTS = 212992
N_REP = 4


def steps_of(own_key, extent, shards, low, largest):
    def one(dim, parts):
        draws = jax.random.uniform(jax.random.fold_in(jax.random.fold_in(own_key, 6), dim), (parts,), jnp.float32, low / len(shards), largest / len(shards))
        return jnp.repeat(jnp.exp(draws), extent[dim] // parts).reshape((-1,) + (1,) * (len(extent) - dim - 1))

    gain = one(*shards[0])
    for cut in shards[1:]:
        gain = gain * one(*cut)
    return gain


def assign_block(rng, own, number, rows, amount, top, limit, lean):
    ranking = jax.random.permutation(rng, amount)
    packed, usual = portions_of(amount, rows * top, limit, lean, True), portions_of(amount, rows * top, limit, lean, False)
    places = jnp.arange(amount)

    def named(tallies, turn):
        used = int((tallies > 0).sum())
        fixed = max(1, used // 4)
        passed = fixed + (places - fixed + turn * (used - fixed)) % max(1, amount - fixed)
        return jnp.zeros((amount,), jnp.int32).at[ranking[jnp.where(places < fixed, places, passed)]].set(jnp.asarray(tallies, jnp.int32))

    tallies = jnp.where(number % 4 == 0, named(packed, number // 4), named(usual, number - number // 4 - 1))
    mixed = jax.random.permutation(jax.random.fold_in(own, 3), amount)
    source_of, sink = mixed[0:amount // 2 * 2:2], mixed[1:amount // 2 * 2:2]
    room = jnp.minimum(tallies[source_of] - 1, limit - tallies[sink]) // 2
    room = jnp.where((source_of == ranking[0]) | (sink == ranking[0]) | (tallies[sink] == 0), 0, jnp.maximum(room, 0))
    passed = jax.random.randint(jax.random.fold_in(own, 4), (amount // 2,), 0, 1 << 20) % (room + 1)
    tallies = tallies.at[source_of].add(-passed).at[sink].add(passed)
    labels = jnp.searchsorted(jnp.cumsum(tallies), jnp.arange(rows * top), side="right").astype(jnp.int32)
    table = labels.reshape(top, rows).T
    table = table[jax.random.permutation(jax.random.fold_in(own, 1), rows)]
    turn = jax.random.randint(jax.random.fold_in(own, 2), (rows, 1), 0, top)
    return jnp.take_along_axis(table, (jnp.arange(top)[None, :] + turn) % top, axis=1)


def portions_of(amount, total, most, skew, full):
    loads = [(1 << 20) // math.isqrt(rank ** skew) + 1 for rank in range(1, amount + 1)]
    largest = most if full else min(most, max(-(-total // amount), total * loads[0] // sum(loads)))
    least = 1 if total - largest >= amount - 1 else 0
    counts, rest = [largest] + [least] * (amount - 1), total - largest - least * (amount - 1)
    while rest > 0:
        candidates = [i for i in range(1, amount) if counts[i] < largest] or [i for i in range(1, amount) if counts[i] < most]
        pool, budget = sum([loads[i] for i in candidates]), rest
        for i in candidates:
            addition = min(most - counts[i], max(1, budget * loads[i] // pool), rest)
            counts[i] = counts[i] + addition
            rest = rest - addition
    return np.array(counts)


def normal_values(own_key, dims, deviation, bound, cuts=(), kind=jnp.bfloat16):
    entries = deviation * jax.random.normal(own_key, dims, jnp.float32)
    if cuts:
        entries = entries * steps_of(own_key, dims, cuts, -0.22, 0.18)
    return jnp.clip(entries, -bound, bound).astype(kind)


def setup_inputs(seed: int = 0) -> dict:
    keys = jax.random.split(jax.random.key(seed), 10)
    d_out = normal_values(keys[0], (TOKENS, D), 1.0, 6.0, ((0, 256),))
    saved_input = normal_values(keys[1], (TOKENS, D), 1.0, 6.0, ((0, 256),))
    routes_keys = jax.random.split(jax.random.fold_in(keys[2], 1), TOKENS // T_DEV)
    routes_turns = jax.random.permutation(jax.random.fold_in(keys[2], 3), TOKENS // T_DEV)
    routes = jax.vmap(lambda own, number: assign_block(jax.random.fold_in(keys[2], 2), own, number, T_DEV, EXPERTS, TOP, CAP, 2))(routes_keys, routes_turns).reshape((TOKENS, TOP))
    probs = jnp.clip(jnp.exp(math.log(0.5) - 2.306499 * jax.random.uniform(keys[3], (TOKENS, TOP), jnp.float32) ** steps_of(keys[3], (TOKENS, TOP), ((0, 256),), -0.2, 0.2)), 0.049804688, 0.5).astype(jnp.bfloat16)
    gate_pre = normal_values(keys[4], (ALL_SLOTS, H), 1.0, 6.0, ((0, 256),))
    up_pre = normal_values(keys[5], (ALL_SLOTS, H), 1.0, 6.0, ((0, 256),))
    gate_weight = normal_values(keys[6], (EXPERTS, H, D), D ** -0.5, 0.125, ((0, 64), (1, 4)))
    up_weight = normal_values(keys[7], (EXPERTS, H, D), D ** -0.5, 0.125, ((0, 64), (1, 4)))
    down_weight = normal_values(keys[8], (EXPERTS, H, D), H ** -0.5, 0.21875, ((0, 64), (1, 4)))
    return {"d_out": d_out, "saved_input": saved_input, "routes": routes, "probs": probs, "gate_pre": gate_pre, "up_pre": up_pre, "gate_weight": gate_weight, "up_weight": up_weight, "down_weight": down_weight}


def contract_rows(left, right):
    return lax.dot_general(left, right, (((0,), (0,)), ((), ())), preferred_element_type=jnp.float32)


def contract_cols(left, right):
    return lax.dot_general(left, right, (((1,), (1,)), ((), ())), preferred_element_type=jnp.float32)


def route_slots(routes):
    blocks = routes.reshape(N_REP * EXPERTS, T_DEV * TOP)
    expert_ids = jnp.arange(EXPERTS, dtype=jnp.int32)
    onehot = (blocks[:, :, None] == expert_ids[None, None, :]).astype(jnp.int32)
    running = jnp.cumsum(onehot, axis=1) - 1
    position = jnp.sum(running * onehot, axis=2).astype(jnp.int32)
    number = jnp.arange(N_REP * EXPERTS, dtype=jnp.int32)
    replica = number // EXPERTS
    source = number % EXPERTS
    slot_index = ((replica[:, None] * EXPERTS + blocks) * EXPERTS + source[:, None]) * CAP + position
    return slot_index.reshape(-1).astype(jnp.int32)


def expert_backward(slot_grad, slot_input, weight, pre_gate, pre_up, gate_full, up_full, down_full):
    down_back = contract_cols(slot_grad, down_full)
    gate_val = pre_gate.astype(jnp.float32)
    up_val = pre_up.astype(jnp.float32)
    logistic = jax.nn.sigmoid(gate_val)
    silu_gate = gate_val * logistic
    activation = (silu_gate * up_val).astype(jnp.bfloat16)
    prob_grad = jnp.sum(down_back * activation.astype(jnp.float32), axis=1).astype(jnp.bfloat16)
    scaled = weight[:, None] * down_back
    gate_back = (scaled * up_val * logistic * (1.0 + gate_val * (1.0 - logistic))).astype(jnp.bfloat16)
    up_back = (scaled * silu_gate).astype(jnp.bfloat16)
    input_grad = (jnp.dot(gate_back, gate_full, preferred_element_type=jnp.float32)
                  + jnp.dot(up_back, up_full, preferred_element_type=jnp.float32)).astype(jnp.bfloat16)
    weighted_grad = (weight[:, None] * slot_grad.astype(jnp.float32)).astype(jnp.bfloat16)
    part_down = contract_rows(activation, weighted_grad)
    part_gate = contract_rows(gate_back, slot_input)
    part_up = contract_rows(up_back, slot_input)
    return input_grad, prob_grad, part_gate, part_up, part_down


def reference(d_out, saved_input, routes, probs, gate_pre, up_pre, gate_weight, up_weight, down_weight):
    route_total = TOKENS * TOP
    slot_index = route_slots(routes)
    slot_owner = jnp.full((ALL_SLOTS,), route_total, jnp.int32).at[slot_index].set(jnp.arange(route_total, dtype=jnp.int32))
    grad_ext = jnp.concatenate([d_out, jnp.zeros((1, D), jnp.bfloat16)], axis=0)
    input_ext = jnp.concatenate([saved_input, jnp.zeros((1, D), jnp.bfloat16)], axis=0)
    prob_ext = jnp.concatenate([probs.reshape(-1), jnp.zeros((1,), jnp.bfloat16)], axis=0)

    def per_expert(state_pair, expert):
        token_acc, prob_acc = state_pair
        gate_full = gate_weight[expert]
        up_full = up_weight[expert]
        down_full = down_weight[expert]
        sum_gate = jnp.zeros((H, D), jnp.float32)
        sum_up = jnp.zeros((H, D), jnp.float32)
        sum_down = jnp.zeros((H, D), jnp.float32)
        for replica in range(N_REP):
            offset = ((replica * EXPERTS + expert) * EXPERTS * CAP).astype(jnp.int32)
            owners = lax.dynamic_slice_in_dim(slot_owner, offset, SLOTS)
            token_id = (owners // TOP).astype(jnp.int32)
            slot_grad = grad_ext[token_id]
            slot_input = input_ext[token_id]
            weight = prob_ext[owners].astype(jnp.float32)
            pre_gate = lax.dynamic_slice_in_dim(gate_pre, offset, SLOTS)
            pre_up = lax.dynamic_slice_in_dim(up_pre, offset, SLOTS)
            input_grad, prob_grad, part_gate, part_up, part_down = expert_backward(
                slot_grad, slot_input, weight, pre_gate, pre_up, gate_full, up_full, down_full)
            token_acc = token_acc.at[token_id].add(input_grad.astype(jnp.float32))
            prob_acc = prob_acc.at[owners].set(prob_grad)
            sum_gate = sum_gate + part_gate.astype(jnp.bfloat16).astype(jnp.float32)
            sum_up = sum_up + part_up.astype(jnp.bfloat16).astype(jnp.float32)
            sum_down = sum_down + part_down.astype(jnp.bfloat16).astype(jnp.float32)
        return (token_acc, prob_acc), (sum_gate, sum_up, sum_down)

    start_pair = (jnp.zeros((TOKENS + 1, D), jnp.float32), jnp.zeros((route_total + 1,), jnp.bfloat16))
    final_pair, grads = lax.scan(per_expert, start_pair, jnp.arange(EXPERTS, dtype=jnp.int32))
    token_acc, prob_acc = final_pair
    d_tokens = token_acc[:TOKENS].astype(jnp.bfloat16)
    d_probs = prob_acc[:route_total].reshape(TOKENS, TOP)
    return d_tokens, d_probs, grads[0], grads[1], grads[2]
```

```python
import jax
import jax.numpy as jnp
from jax import lax
from jax.experimental import pallas as pl
from jax.experimental.pallas import tpu as pltpu
from jax.sharding import PartitionSpec as P

NX, NY, NZ, NC = 4, 4, 8, 2
NG = NY * NC
CAP, TOP = 13, 6
T = 128
D, H = 2048, 704
HS = H // NX
NK = 4
CW = D // NK
GR = 128
GS = 112
S = NG * GR
HALF = D // 2
DOWN, GATE, UP = 0, 1, 2
MESH = pl.DeviceIdType.MESH
F32, BF16 = jnp.float32, jnp.bfloat16
Y_OFFSETS = [(dy, dc) for dy in range(NY) for dc in range(NC) if (dy, dc) != (0, 0)]


def nn(a, b):
    return jnp.dot(a, b, preferred_element_type=F32)


def nt(a, b):
    return lax.dot_general(a, b, (((1,), (1,)), ((), ())), preferred_element_type=F32)


def iota(shape, dim):
    return lax.broadcasted_iota(jnp.int32, shape, dim)


def div13(r):
    return (r * 79) >> 10


def body(
    d_out, saved, routes_t, probs_t, gpre, upre, dw, gw, uw,
    dtok, dprob, dg, gg, ug,
    wfull, zb, ys, slots, oh, oht, gp, up, aw, gbt, ubt, pt0, zrecv, xrel, xfin, stage, psum,
    meta_out, meta_in, ws, wr, ps, pr, dps, dpr,
    ag_s, ag_r, rs_s, rs_r, zs_s, zs_r, tz_s, tz_r, yd_s, yd_r, yr_s, yr_r,
    m_s, m_r, w_s, w_r, p_s, p_r, q_s, q_r, loc, out_sem,
):
    x = lax.axis_index("rep")
    ep = lax.axis_index("ep")
    core = lax.rem(ep, NC)
    z = lax.rem(ep // NC, NZ)
    y = ep // (NC * NZ)
    me_g = y * NC + core

    def at_x(d):
        return lax.rem(x + d + NX, NX)

    def at_z(d):
        return lax.rem(z + d + NZ, NZ)

    def dev_x(d):
        return (at_x(d), ep)

    def dev_z(d):
        return (x, (y * NZ + at_z(d)) * NC + core)

    def dev_y(i):
        dy, dc = Y_OFFSETS[i]
        y2, c2 = lax.rem(y + dy, NY), lax.rem(core + dc, NC)
        return y2 * NC + c2, (x, (y2 * NZ + z) * NC + c2)

    def remote(src, dst, send, recv, device):
        return pltpu.make_async_remote_copy(
            src_ref=src, dst_ref=dst, send_sem=send, recv_sem=recv,
            device_id=device, device_id_type=MESH,
        )

    barrier = pltpu.get_barrier_semaphore()
    peers = [dev_x(1), dev_x(-1)] + [dev_z(d) for d in range(1, NZ)]
    peers += [dev_y(i)[1] for i in range(len(Y_OFFSETS))]
    for device in peers:
        pl.semaphore_signal(barrier, inc=1, device_id=device, device_id_type=MESH)

    own = []
    for a, ref in enumerate((d_out, saved)):
        for k in range(NK):
            own.append(
                pltpu.make_async_copy(
                    ref.at[:, pl.ds(k * CW, CW)], zb.at[a, k, z], loc.at[a * NK + k]
                )
            )
    for cp in own:
        cp.start()
    shards = (dw, gw, uw)
    own_w = [pltpu.make_async_copy(shards[a], wfull.at[a, x], loc.at[2 * NK + a]) for a in range(3)]
    for cp in own_w:
        cp.start()
    pl.semaphore_wait(barrier, len(peers))

    def ag_copy(a, i):
        if i == 0:
            return remote(shards[a], wfull.at[a, x], ag_s.at[a, 0], ag_r.at[a, 0], dev_x(1))
        if i == 1:
            return remote(shards[a], wfull.at[a, x], ag_s.at[a, 1], ag_r.at[a, 1], dev_x(-1))
        if i == 2:
            ref = wfull.at[a, at_x(-1), :, pl.ds(0, HALF)]
            return remote(ref, ref, ag_s.at[a, 2], ag_r.at[a, 2], dev_x(1))
        ref = wfull.at[a, at_x(1), :, pl.ds(HALF, HALF)]
        return remote(ref, ref, ag_s.at[a, 3], ag_r.at[a, 3], dev_x(-1))

    def ag_start(a):
        ag_copy(a, 0).start()
        ag_copy(a, 1).start()

    def ag_relay(a):
        ag_copy(a, 0).wait_recv()
        ag_copy(a, 2).start()
        ag_copy(a, 1).wait_recv()
        ag_copy(a, 3).start()

    def ag_finish(a):
        ag_copy(a, 2).wait_recv()
        ag_copy(a, 3).wait_recv()
        own_w[a].wait()
        for i in range(4):
            ag_copy(a, i).wait_send()

    def hops(k):
        return (4, 3) if k % 2 == 0 else (3, 4)

    def zag_copy(a, k, way, s):
        sign = 1 if way == 0 else -1
        i = s if way == 0 else hops(k)[0] + s
        ref = zb.at[a, k, at_z(-sign * s)]
        return remote(ref, ref, zs_s.at[a, k, i], zs_r.at[a, k, i], dev_z(sign))

    def zag_step(n, s):
        a, k = n // NK, n % NK
        if s == 0:
            own[n].wait()
        for way in range(2):
            if 1 <= s <= hops(k)[way]:
                zag_copy(a, k, way, s - 1).wait_recv()
            if s < hops(k)[way]:
                zag_copy(a, k, way, s).start()

    def zag_sent(n):
        a, k = n // NK, n % NK
        for way in range(2):
            for s in range(hops(k)[way]):
                zag_copy(a, k, way, s).wait_send()

    def yd_copy(a, k, i):
        g, device = dev_y(i)
        return remote(
            ys.at[k % 2, g, pl.ds(0, GS)], slots.at[a, k, me_g, pl.ds(0, GS)],
            yd_s.at[a, k, i], yd_r.at[a, k, i], device,
        )

    def dispatch(n):
        a, k = n // NK, n % NK
        zag_sent(n)
        if n >= 2:
            for i in range(7):
                yd_copy((n - 2) // NK, (n - 2) % NK, i).wait_send()
        rows = nn(oh[...].reshape(S, NZ * T), zb[a, k].reshape(NZ * T, CW))
        ys[k % 2] = rows.astype(BF16).reshape(NG, GR, CW)
        for i in range(7):
            yd_copy(a, k, i).start()
        slots[a, k, me_g] = ys[k % 2, me_g]

    def m_copy(d):
        return remote(meta_out.at[at_z(d)], meta_in.at[z], m_s.at[d - 1], m_r.at[d - 1], dev_z(d))

    def w_copy(i):
        g, device = dev_y(i)
        return remote(ws.at[g], wr.at[me_g], w_s.at[i], w_r.at[i], device)

    def p_copy(i):
        g, device = dev_y(i)
        return remote(ps.at[g], pr.at[me_g], p_s.at[i], p_r.at[i], device)

    def q_copy(d):
        return remote(dps.at[at_z(d)], dpr.at[z], q_s.at[d - 1], q_r.at[d - 1], dev_z(d))

    def expert_of_row():
        q = iota((NZ * NG, T), 0)
        return (((q >> 1) & 3) * NZ + (q >> 3)) * NC + (q & 1)

    def send_meta():
        ids = expert_of_row()
        hit_sum = jnp.zeros((NZ * NG, T), F32)
        prob_sum = jnp.zeros((NZ * NG, T), F32)
        for k in range(TOP):
            hit = ids == routes_t[k : k + 1, :]
            hit_sum = hit_sum + jnp.where(hit, 1.0, 0.0)
            prob_sum = prob_sum + jnp.where(hit, probs_t[k : k + 1, :].astype(F32), 0.0)
        before = jnp.where(iota((T, T), 0) < iota((T, T), 1), 1.0, 0.0).astype(BF16)
        rank = hit_sum * (nn(hit_sum.astype(BF16), before) + 1.0)
        for d in range(NZ):
            part = slice(d * NG, (d + 1) * NG)
            meta_out[d] = jnp.concatenate([rank[part], prob_sum[part]], axis=0).astype(BF16)
        for d in range(1, NZ):
            m_copy(d).start()
        meta_in[z] = meta_out[z]

    def permute_slots():
        n = iota((1, S), 1)
        g, r = n >> 7, n & 127
        zr = div13(r)
        slot = (((g >> 1) * NZ + zr) * NC + (g & 1)) * CAP + (r - zr * CAP)
        slot = jnp.where(r < NZ * CAP, slot, -1)
        perm = jnp.where(iota((NG * NZ * CAP, S), 0) == slot, 1.0, 0.0).astype(BF16)
        for j in range(NX):
            gp[j] = nn(gpre[pl.ds(j * HS, HS), :], perm).astype(BF16)
            up[j] = nn(upre[pl.ds(j * HS, HS), :], perm).astype(BF16)

    def build_tables():
        for d in range(1, NZ):
            m_copy(d).wait()
        table = jnp.concatenate([meta_in[d].astype(F32) for d in range(NZ)], axis=1)
        r = iota((GR, NZ * T), 0)
        zr = div13(r)
        key = jnp.where(
            (zr == (iota((GR, NZ * T), 1) >> 7)) & (r < NZ * CAP), r - zr * CAP + 1, -1
        ).astype(F32)
        for g in range(NG):
            oh[g] = jnp.where(table[g : g + 1, :] == key, 1.0, 0.0).astype(BF16)
        table16 = table.astype(BF16)
        for g in range(NG):
            rows = nt(table16, oh[g])
            ws[g] = jnp.broadcast_to(rows[NG + g : NG + g + 1, :], (16, GR)).astype(BF16)
        for i in range(7):
            w_copy(i).start()
        wr[me_g] = ws[me_g]

    def transpose_tables():
        for g in range(NG):
            oht[:, pl.ds(g * GR, GR)] = oh[g].T

    def tile_down(i):
        j = at_x(2 + i)
        back = jnp.zeros((HS, S), F32)
        for k in range(NK):
            back = back + nt(wfull[DOWN, j, :, pl.ds(k * CW, CW)], slots[0, k].reshape(S, CW))
        weight = jnp.concatenate([wr[g][0:1, :].astype(F32) for g in range(NG)], axis=1)
        gate_val, up_val = gp[j].astype(F32), up[j].astype(F32)
        logistic = 1.0 / (1.0 + jnp.exp(-gate_val))
        silu = gate_val * logistic
        act = (silu * up_val).astype(BF16).astype(F32)
        total = jnp.sum(back * act, axis=0, keepdims=True)
        if i == 0:
            psum[0:1, :] = total
        else:
            psum[0:1, :] = psum[0:1, :] + total
        scaled = weight * back
        aw[j] = (weight * act).astype(BF16)
        gp[j] = (scaled * up_val * logistic * (1.0 + gate_val * (1.0 - logistic))).astype(BF16)
        up[j] = (scaled * silu).astype(BF16)
        for k in range(NK):
            pt0[j, :, pl.ds(k * CW, CW)] = nn(aw[j], slots[0, k].reshape(S, CW)).astype(BF16)

    def tile_part(j, left, dst):
        for k in range(NK):
            dst[j, :, pl.ds(k * CW, CW)] = nn(left[j], slots[1, k].reshape(S, CW)).astype(BF16)

    parts = (pt0, wfull.at[DOWN], wfull.at[GATE])
    low, high = pl.ds(0, HALF), pl.ds(HALF, HALF)

    def rs_copy(a, i):
        p = parts[a]
        if i == 0:
            src, dst, device = p.at[at_x(2), :, low], xrel.at[a, 0], dev_x(1)
        elif i == 1:
            src, dst, device = p.at[at_x(2), :, high], xrel.at[a, 1], dev_x(-1)
        elif i == 2:
            src, dst, device = p.at[at_x(1), :, high], xfin.at[a, 0, :, high], dev_x(1)
        elif i == 3:
            src, dst, device = p.at[at_x(-1), :, low], xfin.at[a, 1, :, low], dev_x(-1)
        elif i == 4:
            src, dst, device = p.at[at_x(1), :, low], xfin.at[a, 0, :, low], dev_x(1)
        else:
            src, dst, device = p.at[at_x(-1), :, high], xfin.at[a, 1, :, high], dev_x(-1)
        return remote(src, dst, rs_s.at[a, i], rs_r.at[a, i], device)

    def rs_start(a):
        for i in range(4):
            rs_copy(a, i).start()

    def rs_relay(a):
        p = parts[a]
        rs_copy(a, 0).wait_recv()
        right = at_x(1)
        p[right, :, low] = (p[right, :, low].astype(F32) + xrel[a, 0].astype(F32)).astype(BF16)
        rs_copy(a, 4).start()
        rs_copy(a, 1).wait_recv()
        left = at_x(-1)
        p[left, :, high] = (p[left, :, high].astype(F32) + xrel[a, 1].astype(F32)).astype(BF16)
        rs_copy(a, 5).start()

    def out_copy(a):
        return pltpu.make_async_copy(stage, (dg, gg, ug)[a], out_sem)

    def rs_finish(a):
        for i in range(2, 6):
            rs_copy(a, i).wait_recv()
        if a != DOWN:
            out_copy(a - 1).wait()
        stage[...] = parts[a][x].astype(F32) + xfin[a, 0].astype(F32) + xfin[a, 1].astype(F32)
        out_copy(a).start()
        for i in range(6):
            rs_copy(a, i).wait_send()

    def yr_copy(k, i):
        g, device = dev_y(i)
        return remote(
            ys.at[k % 2, g, pl.ds(0, GS)], zb.at[0, k, me_g, pl.ds(0, GS)],
            yr_s.at[k, i], yr_r.at[k, i], device,
        )

    def give_back(k):
        cols = pl.ds(k * CW, CW)
        if k >= 2:
            for i in range(7):
                yr_copy(k - 2, i).wait_send()
        else:
            for i in range(7):
                yd_copy(1, k + 2, i).wait_send()
        rows = nn(gbt[...], wfull[GATE, :, :, cols].reshape(H, CW))
        rows = rows + nn(ubt[...], wfull[UP, :, :, cols].reshape(H, CW))
        ys[k % 2] = rows.astype(BF16).reshape(NG, GR, CW)
        for i in range(7):
            yr_copy(k, i).start()
        zb[0, k, me_g] = ys[k % 2, me_g]

    def tz_copy(k, way, s):
        sign = 1 if way == 0 else -1
        count = hops(k)[way]
        i = s if way == 0 else hops(k)[0] + s
        return remote(
            zb.at[1, k, at_z(sign * (count - s))], zrecv.at[k, i],
            tz_s.at[k, i], tz_r.at[k, i], dev_z(sign),
        )

    def combine(k):
        for i in range(7):
            yr_copy(k, i).wait_recv()
        total = nn(oht[...], zb[0, k].reshape(S, CW))
        zb[1, k] = total.astype(BF16).reshape(NZ, T, CW)

    def tz_step(k, s):
        if s == 0:
            combine(k)
        for way in range(2):
            sign, count = (1 if way == 0 else -1), hops(k)[way]
            base = 0 if way == 0 else hops(k)[0]
            if 1 <= s <= count:
                tz_copy(k, way, s - 1).wait_recv()
            if s < count:
                if s >= 1:
                    to = at_z(sign * (count - s))
                    zb[1, k, to] = (
                        zb[1, k, to].astype(F32) + zrecv[k, base + s - 1].astype(F32)
                    ).astype(BF16)
                tz_copy(k, way, s).start()
        if s == 4:
            first, second = hops(k)
            total = zb[1, k, z].astype(F32) + zrecv[k, first - 1].astype(F32)
            total = total + zrecv[k, first + second - 1].astype(F32)
            dtok[:, pl.ds(k * CW, CW)] = total.astype(BF16)

    send_meta()
    ag_start(0)
    zag_step(0, 0)
    ag_start(1)
    zag_step(1, 0)
    for a in range(2):
        for k in range(NK):
            slots[a, k, :, pl.ds(GS, GR - GS), :] = jnp.zeros((NG, GR - GS, CW), BF16)

    for slot in range(1, 2 * NK + 4):
        for s in range(4, -1, -1):
            n = slot - s
            if 0 <= n < 2 * NK and (n, s) not in ((0, 0), (1, 0)):
                zag_step(n, s)
        if slot == 1:
            build_tables()
        if slot == 2:
            permute_slots()
            ag_relay(0)
            ag_start(2)
        if slot == 3:
            transpose_tables()
        if slot >= 4:
            dispatch(slot - 4)
        if slot == 5:
            ag_relay(1)
        if slot == 7:
            ag_relay(2)
            ag_finish(0)
        if slot == 8:
            for i in range(7):
                w_copy(i).wait()
        if slot == 9:
            for k in range(NK):
                for i in range(7):
                    yd_copy(0, k, i).wait_recv()
            tile_down(0)
        if slot == 10:
            tile_down(1)
            tile_down(2)
    tile_down(3)
    rs_start(DOWN)

    for g in range(NG):
        cols = pl.ds(g * GR, GR)
        ps[g] = jnp.broadcast_to(psum[0:1, cols], (16, GR)).astype(BF16)
        gbt[cols, :] = gp[:, :, cols].reshape(H, GR).T
        ubt[cols, :] = up[:, :, cols].reshape(H, GR).T
    for i in range(7):
        p_copy(i).start()
    pr[me_g] = ps[me_g]
    ag_finish(1)
    ag_finish(2)
    for k in range(NK):
        give_back(k)
    for k in range(NK):
        for i in range(7):
            yd_copy(1, k, i).wait_recv()
    for i in range(NX):
        tile_part(at_x(2 + i), gp, parts[GATE])
    rs_start(GATE)
    rs_relay(DOWN)
    for i in range(NX):
        tile_part(at_x(2 + i), up, parts[UP])
    rs_start(UP)

    for i in range(7):
        p_copy(i).wait()
    dense = []
    for g in range(NG):
        dense.append(nn(pr[g], oh[g])[0:1, :])
    dense = jnp.concatenate(dense, axis=0)
    for d in range(NZ):
        part = dense[:, d * T : (d + 1) * T]
        dps[d] = jnp.concatenate([part, jnp.zeros((16 - NG, T), F32)], axis=0).astype(BF16)
    for d in range(1, NZ):
        q_copy(d).start()
    dpr[z] = dps[z]

    for slot in range(NK + 4):
        for s in range(4, -1, -1):
            k = slot - s
            if 0 <= k < NK:
                tz_step(k, s)
        if slot == 1:
            rs_finish(DOWN)
        if slot == 3:
            rs_relay(GATE)
            for d in range(1, NZ):
                q_copy(d).wait()
            ids = expert_of_row()
            table = jnp.concatenate([dpr[d][0:NG, :].astype(F32) for d in range(NZ)], axis=0)
            rows = []
            for k in range(TOP):
                hit = ids == routes_t[k : k + 1, :]
                rows.append(jnp.sum(jnp.where(hit, table, 0.0), axis=0, keepdims=True))
            dprob[...] = jnp.concatenate(rows, axis=0).astype(BF16)
        if slot == 5:
            rs_relay(UP)
        if slot == 6:
            rs_finish(GATE)
    rs_finish(UP)
    for k in range(NK):
        for way in range(2):
            for s in range(hops(k)[way]):
                tz_copy(k, way, s).wait_send()
    for k in (NK - 2, NK - 1):
        for i in range(7):
            yr_copy(k, i).wait_send()
    out_copy(UP).wait()


def on_device(
    d_out, saved_input, routes, probs, gate_pre, up_pre, gate_weight, up_weight, down_weight
):
    any_space = pl.BlockSpec(memory_space=pl.ANY)
    vmem = pl.BlockSpec(memory_space=pltpu.VMEM)
    dma = pltpu.SemaphoreType.DMA
    weight_grad = jax.ShapeDtypeStruct((HS, D), F32)
    d_tokens, d_probs, down_grad, gate_grad, up_grad = pl.pallas_call(
        body,
        out_shape=(
            jax.ShapeDtypeStruct((T, D), BF16),
            jax.ShapeDtypeStruct((TOP, T), BF16),
            weight_grad,
            weight_grad,
            weight_grad,
        ),
        in_specs=[any_space] * 2 + [vmem] * 4 + [any_space] * 3,
        out_specs=(vmem, vmem, any_space, any_space, any_space),
        scratch_shapes=[
            pltpu.VMEM((3, NX, HS, D), BF16),
            pltpu.VMEM((2, NK, NZ, T, CW), BF16),
            pltpu.VMEM((2, NG, GR, CW), BF16),
            pltpu.VMEM((2, NK, NG, GR, CW), BF16),
            pltpu.VMEM((NG, GR, NZ * T), BF16),
            pltpu.VMEM((NZ * T, S), BF16),
            pltpu.VMEM((NX, HS, S), BF16),
            pltpu.VMEM((NX, HS, S), BF16),
            pltpu.VMEM((NX, HS, S), BF16),
            pltpu.VMEM((S, H), BF16),
            pltpu.VMEM((S, H), BF16),
            pltpu.VMEM((NX, HS, D), BF16),
            pltpu.VMEM((NK, 7, T, CW), BF16),
            pltpu.VMEM((3, 2, HS, HALF), BF16),
            pltpu.VMEM((3, 2, HS, D), BF16),
            pltpu.VMEM((HS, D), F32),
            pltpu.VMEM((8, S), F32),
        ]
        + [pltpu.VMEM((8, 16, T), BF16)] * 8
        + [dma((3, 4)), dma((3, 4)), dma((3, 6)), dma((3, 6))]
        + [dma((2, NK, 7)), dma((2, NK, 7)), dma((NK, 7)), dma((NK, 7))]
        + [dma((2, NK, 7)), dma((2, NK, 7)), dma((NK, 7)), dma((NK, 7))]
        + [dma((7,))] * 8
        + [dma((2 * NK + 3,)), dma],
        compiler_params=pltpu.CompilerParams(
            collective_id=0, has_side_effects=True, vmem_limit_bytes=62 * 2**20
        ),
        cost_estimate=pl.CostEstimate(
            flops=16 * 10**9, bytes_accessed=20 * 10**6, transcendentals=10**6
        ),
    )(
        d_out, saved_input, routes.T, probs.T, gate_pre.T, up_pre.T,
        down_weight[0], gate_weight[0], up_weight[0],
    )
    return d_tokens, d_probs.T, gate_grad[None], up_grad[None], down_grad[None]


def solution(mesh):
    token = P(("rep", "ep"), None)
    weight = P("ep", "rep", None)
    return jax.shard_map(
        on_device,
        mesh=mesh,
        in_specs=(token,) * 6 + (weight,) * 3,
        out_specs=(token, token, weight, weight, weight),
        check_vma=False,
    )
```

```python
import jax
import jax.numpy as jnp
from jax import lax
from jax.experimental import pallas as pl
from jax.experimental.pallas import tpu as pltpu
from jax.sharding import PartitionSpec as P

NX, NY, NZ, NC = 4, 4, 8, 2
NG = NY * NC
CAP, TOP = 13, 6
T = 128
D, H = 2048, 704
HS = H // NX
NK = 4
CW = D // NK
THERE = [(0, 0, 256), (0, 256, 256), (0, 512, 512), (0, 1024, 512), (0, 1536, 512)]
THERE += [(1, 0, 512), (1, 512, 512), (1, 1024, 512), (1, 1536, 512)]
BACK = [(0, 512), (512, 512), (1024, 512), (1536, 256), (1792, 256)]
NT, NB, NYS = len(THERE), len(BACK), 4
ORDER = [0, 1, 2, 3, 4, 5, 6, NT, NT + 1, NT + 2, 7, NT + 3, 8, NT + 4]
TURN = {chunk: place for place, chunk in enumerate(ORDER)}
GR = 128
GS = 112
S = NG * GR
HALF = D // 2
DOWN, GATE, UP = 0, 1, 2
MESH = pl.DeviceIdType.MESH
F32, BF16 = jnp.float32, jnp.bfloat16
Y_OFFSETS = [(dy, dc) for dy in range(NY) for dc in range(NC) if (dy, dc) != (0, 0)]


def nn(a, b):
    return jnp.dot(a, b, preferred_element_type=F32)


def nt(a, b):
    return lax.dot_general(a, b, (((1,), (1,)), ((), ())), preferred_element_type=F32)


def iota(shape, dim):
    return lax.broadcasted_iota(jnp.int32, shape, dim)


def div13(r):
    return (r * 79) >> 10


def body(
    d_out, saved, routes_t, probs_t, gpre, upre, dw, gw, uw,
    dtok, dprob, dg, gg, ug,
    wfull, zb, ys, slots, oh, oht, gp, up, aw, gbt, ubt, pt0, pt2, zrecv, xrel, xfin, stage, psum,
    meta_out, meta_in, ws, wr, ps, pr, dps, dpr,
    ag_s, ag_r, rs_s, rs_r, zs_s, zs_r, tz_s, tz_r, yd_s, yd_r, yr_s, yr_r,
    m_s, m_r, w_s, w_r, p_s, p_r, q_s, q_r, loc, out_sem,
):
    x = lax.axis_index("rep")
    ep = lax.axis_index("ep")
    core = lax.rem(ep, NC)
    z = lax.rem(ep // NC, NZ)
    y = ep // (NC * NZ)
    me_g = y * NC + core

    def at_x(d):
        return lax.rem(x + d + NX, NX)

    def at_z(d):
        return lax.rem(z + d + NZ, NZ)

    def dev_x(d):
        return (at_x(d), ep)

    def dev_z(d):
        return (x, (y * NZ + at_z(d)) * NC + core)

    def dev_y(i):
        dy, dc = Y_OFFSETS[i]
        y2, c2 = lax.rem(y + dy, NY), lax.rem(core + dc, NC)
        return y2 * NC + c2, (x, (y2 * NZ + z) * NC + c2)

    def remote(src, dst, send, recv, device):
        return pltpu.make_async_remote_copy(
            src_ref=src, dst_ref=dst, send_sem=send, recv_sem=recv,
            device_id=device, device_id_type=MESH,
        )

    barrier = pltpu.get_barrier_semaphore()
    peers = [dev_x(1), dev_x(-1)] + [dev_z(d) for d in range(1, NZ)]
    peers += [dev_y(i)[1] for i in range(len(Y_OFFSETS))]
    for device in peers:
        pl.semaphore_signal(barrier, inc=1, device_id=device, device_id_type=MESH)

    own = []
    for n, (a, col, width) in enumerate(THERE):
        cols = pl.ds(col, width)
        ref = (d_out, saved)[a]
        own.append(pltpu.make_async_copy(ref.at[:, cols], zb.at[a, z, :, cols], loc.at[n]))
    for cp in own:
        cp.start()
    shards = (dw, gw, uw)
    own_w = [pltpu.make_async_copy(shards[a], wfull.at[a, x], loc.at[NT + a]) for a in range(3)]
    for cp in own_w:
        cp.start()
    pl.semaphore_wait(barrier, len(peers))

    def ag_copy(a, i):
        if i == 0:
            return remote(shards[a], wfull.at[a, x], ag_s.at[a, 0], ag_r.at[a, 0], dev_x(1))
        if i == 1:
            return remote(shards[a], wfull.at[a, x], ag_s.at[a, 1], ag_r.at[a, 1], dev_x(-1))
        if i == 2:
            ref = wfull.at[a, at_x(-1), :, pl.ds(0, HALF)]
            return remote(ref, ref, ag_s.at[a, 2], ag_r.at[a, 2], dev_x(1))
        ref = wfull.at[a, at_x(1), :, pl.ds(HALF, HALF)]
        return remote(ref, ref, ag_s.at[a, 3], ag_r.at[a, 3], dev_x(-1))

    def ag_start(a):
        ag_copy(a, 0).start()
        ag_copy(a, 1).start()

    def ag_relay(a):
        ag_copy(a, 0).wait_recv()
        ag_copy(a, 2).start()
        ag_copy(a, 1).wait_recv()
        ag_copy(a, 3).start()

    def ag_finish(a):
        ag_copy(a, 2).wait_recv()
        ag_copy(a, 3).wait_recv()
        own_w[a].wait()
        for i in range(4):
            ag_copy(a, i).wait_send()

    def hops(k):
        return (4, 3) if k % 2 == 0 else (3, 4)

    def zag_copy(n, way, s):
        a, col, width = THERE[n]
        sign = 1 if way == 0 else -1
        i = s if way == 0 else hops(n)[0] + s
        ref = zb.at[a, at_z(-sign * s), :, pl.ds(col, width)]
        return remote(ref, ref, zs_s.at[n, i], zs_r.at[n, i], dev_z(sign))

    def zag_step(n, s):
        if s == 0:
            own[n].wait()
        for way in range(2):
            if 1 <= s <= hops(n)[way]:
                zag_copy(n, way, s - 1).wait_recv()
            if s < hops(n)[way]:
                zag_copy(n, way, s).start()

    def yd_copy(n, i):
        a, col, width = THERE[n]
        g, device = dev_y(i)
        return remote(
            ys.at[TURN[n] % NYS, g, pl.ds(0, GS), pl.ds(0, width)],
            slots.at[a, me_g, pl.ds(0, GS), pl.ds(col, width)],
            yd_s.at[n, i], yd_r.at[n, i], device,
        )

    def sent(chunk):
        for i in range(7):
            (yd_copy(chunk, i) if chunk < NT else yr_copy(chunk - NT, i)).wait_send()

    def free_buffer(chunk):
        if TURN[chunk] >= NYS:
            sent(ORDER[TURN[chunk] - NYS])

    def dispatch(n):
        a, col, width = THERE[n]
        for way in range(2):
            for s in range(hops(n)[way]):
                zag_copy(n, way, s).wait_send()
        free_buffer(n)
        rows = nn(oh[...].reshape(S, NZ * T), zb[a, :, :, pl.ds(col, width)].reshape(NZ * T, width))
        ys[TURN[n] % NYS, :, :, pl.ds(0, width)] = rows.astype(BF16).reshape(NG, GR, width)
        for i in range(7):
            yd_copy(n, i).start()
        slots[a, me_g, :, pl.ds(col, width)] = ys[TURN[n] % NYS, me_g, :, pl.ds(0, width)]

    def arrived(n):
        for i in range(7):
            yd_copy(n, i).wait_recv()

    def m_copy(d):
        return remote(meta_out.at[at_z(d)], meta_in.at[z], m_s.at[d - 1], m_r.at[d - 1], dev_z(d))

    def w_copy(i):
        g, device = dev_y(i)
        return remote(ws.at[g], wr.at[me_g], w_s.at[i], w_r.at[i], device)

    def p_copy(i):
        g, device = dev_y(i)
        return remote(ps.at[g], pr.at[me_g], p_s.at[i], p_r.at[i], device)

    def q_copy(d):
        return remote(dps.at[at_z(d)], dpr.at[z], q_s.at[d - 1], q_r.at[d - 1], dev_z(d))

    def expert_of_row():
        q = iota((NZ * NG, T), 0)
        return (((q >> 1) & 3) * NZ + (q >> 3)) * NC + (q & 1)

    def send_meta():
        ids = expert_of_row()
        hit_sum = jnp.zeros((NZ * NG, T), F32)
        prob_sum = jnp.zeros((NZ * NG, T), F32)
        for k in range(TOP):
            hit = ids == routes_t[k : k + 1, :]
            hit_sum = hit_sum + jnp.where(hit, 1.0, 0.0)
            prob_sum = prob_sum + jnp.where(hit, probs_t[k : k + 1, :].astype(F32), 0.0)
        before = jnp.where(iota((T, T), 0) < iota((T, T), 1), 1.0, 0.0).astype(BF16)
        rank = hit_sum * (nn(hit_sum.astype(BF16), before) + 1.0)
        for d in range(NZ):
            part = slice(d * NG, (d + 1) * NG)
            meta_out[d] = jnp.concatenate([rank[part], prob_sum[part]], axis=0).astype(BF16)
        for d in range(1, NZ):
            m_copy(d).start()
        meta_in[z] = meta_out[z]

    def permute_slots():
        def some(cg, carry):
            n = cg * 256 + iota((1, 256), 1)
            g, r = n >> 7, n & 127
            zr = div13(r)
            slot = (((g >> 1) * NZ + zr) * NC + (g & 1)) * CAP + (r - zr * CAP)
            slot = jnp.where(r < NZ * CAP, slot, -1)
            perm = jnp.where(iota((NG * NZ * CAP, 256), 0) == slot, 1.0, 0.0).astype(BF16)
            cols = pl.ds(pl.multiple_of(cg * 256, 256), 256)
            for j in range(NX):
                gp[j, :, cols] = nn(gpre[pl.ds(j * HS, HS), :], perm).astype(BF16)
                up[j, :, cols] = nn(upre[pl.ds(j * HS, HS), :], perm).astype(BF16)
            return carry

        lax.fori_loop(0, S // 256, some, 0)

    def build_tables():
        for d in range(1, NZ):
            m_copy(d).wait()
        table = jnp.concatenate([meta_in[d].astype(F32) for d in range(NZ)], axis=1)
        r = iota((GR, NZ * T), 0)
        zr = div13(r)
        key = jnp.where(
            (zr == (iota((GR, NZ * T), 1) >> 7)) & (r < NZ * CAP), r - zr * CAP + 1, -1
        ).astype(F32)
        for g in range(NG):
            oh[g] = jnp.where(table[g : g + 1, :] == key, 1.0, 0.0).astype(BF16)
        table16 = table.astype(BF16)
        for g in range(NG):
            rows = nt(table16, oh[g])
            ws[g] = jnp.broadcast_to(rows[NG + g : NG + g + 1, :], (16, GR)).astype(BF16)
        for i in range(7):
            w_copy(i).start()
        wr[me_g] = ws[me_g]

    def transpose_tables():
        for g in range(NG):
            oht[:, pl.ds(g * GR, GR)] = oh[g].T

    def slot_weight():
        return jnp.concatenate([wr[g][0:1, :].astype(F32) for g in range(NG)], axis=1)

    def activation(j):
        gate_val, up_val = gp[j].astype(F32), up[j].astype(F32)
        logistic = 1.0 / (1.0 + jnp.exp(-gate_val))
        silu = gate_val * logistic
        return gate_val, up_val, logistic, silu, (silu * up_val).astype(BF16).astype(F32)

    def tile_act(j):
        aw[j] = (slot_weight() * activation(j)[4]).astype(BF16)

    def tile_back(j):
        back = jnp.zeros((HS, S), F32)
        for k in range(NK):
            cols = pl.ds(k * CW, CW)
            back = back + nt(wfull[DOWN, j, :, cols], slots[0, :, :, cols].reshape(S, CW))
        gate_val, up_val, logistic, silu, act = activation(j)
        total = jnp.sum(back * act, axis=0, keepdims=True)
        if j == 0:
            psum[0:1, :] = total
        else:
            psum[0:1, :] = psum[0:1, :] + total
        scaled = slot_weight() * back
        gp[j] = (scaled * up_val * logistic * (1.0 + gate_val * (1.0 - logistic))).astype(BF16)
        up[j] = (scaled * silu).astype(BF16)

    parts = (pt0, wfull.at[DOWN], pt2)
    lefts = (aw, gp, up)

    def rs_copy(a, k, i):
        p, cols = parts[a], pl.ds(k * CW, CW)
        sign = 1 if k % 2 == 0 else -1
        if i == 0:
            src, dst, device = p.at[at_x(2), :, cols], xrel.at[a, :, cols], dev_x(sign)
        elif i == 1:
            src, dst, device = p.at[at_x(-sign), :, cols], xfin.at[a, 1, :, cols], dev_x(-sign)
        else:
            src, dst, device = p.at[at_x(sign), :, cols], xfin.at[a, 0, :, cols], dev_x(sign)
        return remote(src, dst, rs_s.at[a, k, i], rs_r.at[a, k, i], device)

    def part(a, k):
        cols = pl.ds(k * CW, CW)
        for j in range(NX):
            rows = nn(lefts[a][j], slots[min(a, 1), :, :, cols].reshape(S, CW))
            parts[a][j, :, cols] = rows.astype(BF16)
        rs_copy(a, k, 0).start()
        rs_copy(a, k, 1).start()

    def rs_relay(a, k):
        p, cols = parts[a], pl.ds(k * CW, CW)
        to = at_x(1 if k % 2 == 0 else -1)
        rs_copy(a, k, 0).wait_recv()
        p[to, :, cols] = (p[to, :, cols].astype(F32) + xrel[a, :, cols].astype(F32)).astype(BF16)
        rs_copy(a, k, 2).start()

    def out_copy(a, k):
        cols = pl.ds(k * CW, CW)
        return pltpu.make_async_copy(
            stage.at[:, cols], (dg, gg, ug)[a].at[:, cols], out_sem.at[a, k]
        )

    def rs_finish(a, k):
        cols = pl.ds(k * CW, CW)
        rs_copy(a, k, 1).wait_recv()
        rs_copy(a, k, 2).wait_recv()
        if a != DOWN:
            out_copy(a - 1, k).wait()
        total = xfin[a, 0, :, cols].astype(F32) + xfin[a, 1, :, cols].astype(F32)
        stage[:, cols] = parts[a][x, :, cols].astype(F32) + total
        out_copy(a, k).start()
        for i in range(3):
            rs_copy(a, k, i).wait_send()

    def yr_copy(k, i):
        col, width = BACK[k]
        g, device = dev_y(i)
        return remote(
            ys.at[TURN[NT + k] % NYS, g, pl.ds(0, GS), pl.ds(0, width)],
            zb.at[0, me_g, pl.ds(0, GS), pl.ds(col, width)],
            yr_s.at[k, i], yr_r.at[k, i], device,
        )

    def give_back(k):
        col, width = BACK[k]
        cols, slot = pl.ds(col, width), TURN[NT + k] % NYS
        free_buffer(NT + k)
        rows = nn(gbt[...], wfull[GATE, :, :, cols].reshape(H, width))
        rows = rows + nn(ubt[...], wfull[UP, :, :, cols].reshape(H, width))
        ys[slot, :, :, pl.ds(0, width)] = rows.astype(BF16).reshape(NG, GR, width)
        for i in range(7):
            yr_copy(k, i).start()
        zb[0, me_g, :, cols] = ys[slot, me_g, :, pl.ds(0, width)]

    def tz_copy(k, way, s):
        cols = pl.ds(*BACK[k])
        sign = 1 if way == 0 else -1
        count = hops(k)[way]
        i = s if way == 0 else hops(k)[0] + s
        return remote(
            zb.at[1, at_z(sign * (count - s)), :, cols], zrecv.at[i, :, cols],
            tz_s.at[k, i], tz_r.at[k, i], dev_z(sign),
        )

    def combine(k):
        col, width = BACK[k]
        cols = pl.ds(col, width)
        for i in range(7):
            yr_copy(k, i).wait_recv()
        total = nn(oht[...], zb[0, :, :, cols].reshape(S, width))
        zb[1, :, :, cols] = total.astype(BF16).reshape(NZ, T, width)

    def tz_step(k, s):
        cols = pl.ds(*BACK[k])
        if s == 0:
            combine(k)
        for way in range(2):
            sign, count = (1 if way == 0 else -1), hops(k)[way]
            base = 0 if way == 0 else hops(k)[0]
            if 1 <= s <= count:
                tz_copy(k, way, s - 1).wait_recv()
            if s < count:
                if s >= 1:
                    to = at_z(sign * (count - s))
                    zb[1, to, :, cols] = (
                        zb[1, to, :, cols].astype(F32) + zrecv[base + s - 1, :, cols].astype(F32)
                    ).astype(BF16)
                tz_copy(k, way, s).start()
        if s == 4:
            first, second = hops(k)
            total = zb[1, z, :, cols].astype(F32) + zrecv[first - 1, :, cols].astype(F32)
            total = total + zrecv[first + second - 1, :, cols].astype(F32)
            dtok[:, cols] = total.astype(BF16)

    def send_probs():
        for g in range(NG):
            ps[g] = jnp.broadcast_to(psum[0:1, pl.ds(g * GR, GR)], (16, GR)).astype(BF16)
        for i in range(7):
            p_copy(i).start()
        pr[me_g] = ps[me_g]

    def transpose_backs():
        for g in range(NG):
            cols = pl.ds(g * GR, GR)
            gbt[cols, :] = gp[:, :, cols].reshape(H, GR).T
            ubt[cols, :] = up[:, :, cols].reshape(H, GR).T

    def return_probs():
        for i in range(7):
            p_copy(i).wait()
        dense = jnp.concatenate([nn(pr[g], oh[g])[0:1, :] for g in range(NG)], axis=0)
        for d in range(NZ):
            some = dense[:, d * T : (d + 1) * T]
            dps[d] = jnp.concatenate([some, jnp.zeros((16 - NG, T), F32)], axis=0).astype(BF16)
        for d in range(1, NZ):
            q_copy(d).start()
        dpr[z] = dps[z]

    def pick_probs():
        for d in range(1, NZ):
            q_copy(d).wait()
        ids = expert_of_row()
        table = jnp.concatenate([dpr[d][0:NG, :].astype(F32) for d in range(NZ)], axis=0)
        rows = []
        for k in range(TOP):
            hit = ids == routes_t[k : k + 1, :]
            rows.append(jnp.sum(jnp.where(hit, table, 0.0), axis=0, keepdims=True))
        dprob[...] = jnp.concatenate(rows, axis=0).astype(BF16)

    zag_step(0, 0)
    send_meta()
    zag_step(1, 0)
    ag_start(0)
    ag_start(1)
    for a in range(2):
        slots[a, :, pl.ds(GS, GR - GS), :] = jnp.zeros((NG, GR - GS, D), BF16)

    for slot in range(1, NT + 4):
        for s in range(4, -1, -1):
            n = slot - s
            if 0 <= n < NT and (n, s) not in ((0, 0), (1, 0)):
                zag_step(n, s)
                if s == 4 and n < 7:
                    dispatch(n)
        if slot == 2:
            build_tables()
        if slot == 5:
            ag_relay(0)
            ag_start(2)
            ag_relay(1)
            permute_slots()
        if slot == 6:
            for i in range(7):
                w_copy(i).wait()
            for j in range(NX):
                tile_act(j)
        if slot == 7:
            ag_relay(2)
            arrived(0)
            arrived(1)
            part(DOWN, 0)
        if slot == 8:
            arrived(2)
            part(DOWN, 1)
            ag_finish(0)
        if slot == 9:
            arrived(3)
            part(DOWN, 2)
            transpose_tables()
        if slot == 10:
            arrived(4)
            part(DOWN, 3)
            tile_back(0)
            tile_back(1)
        if slot == 11:
            tile_back(2)
            tile_back(3)
            send_probs()
            transpose_backs()
            ag_finish(1)
            ag_finish(2)
            give_back(0)
            give_back(1)
            rs_relay(DOWN, 0)
    give_back(2)
    rs_relay(DOWN, 1)
    arrived(5)
    part(GATE, 0)
    part(UP, 0)
    rs_relay(DOWN, 2)
    dispatch(7)
    rs_relay(DOWN, 3)
    arrived(6)
    part(GATE, 1)
    part(UP, 1)
    return_probs()
    tz_step(0, 0)
    give_back(3)
    tz_step(0, 1)
    tz_step(1, 0)
    dispatch(8)
    rs_relay(GATE, 0)
    rs_relay(UP, 0)
    tz_step(0, 2)
    tz_step(1, 1)
    tz_step(2, 0)
    give_back(4)
    pick_probs()
    rs_relay(GATE, 1)
    rs_relay(UP, 1)
    tz_step(0, 3)
    tz_step(1, 2)
    tz_step(2, 1)
    arrived(7)
    part(GATE, 2)
    part(UP, 2)
    tz_step(0, 4)
    tz_step(1, 3)
    tz_step(2, 2)
    tz_step(3, 0)
    for k in range(NK):
        rs_finish(DOWN, k)
    tz_step(1, 4)
    tz_step(2, 3)
    tz_step(3, 1)
    rs_relay(GATE, 2)
    rs_relay(UP, 2)
    tz_step(2, 4)
    tz_step(3, 2)
    arrived(8)
    part(GATE, 3)
    part(UP, 3)
    tz_step(3, 3)
    tz_step(4, 0)
    for k in range(2):
        rs_finish(GATE, k)
        rs_finish(UP, k)
    tz_step(3, 4)
    tz_step(4, 1)
    rs_relay(GATE, 3)
    rs_relay(UP, 3)
    tz_step(4, 2)
    rs_finish(GATE, 2)
    rs_finish(UP, 2)
    tz_step(4, 3)
    tz_step(4, 4)
    rs_finish(GATE, 3)
    rs_finish(UP, 3)
    for k in range(NB):
        for way in range(2):
            for s in range(hops(k)[way]):
                tz_copy(k, way, s).wait_send()
    for chunk in ORDER[-NYS:]:
        sent(chunk)
    for k in range(NK):
        out_copy(UP, k).wait()


def hand_out(*refs):
    for i in range(5):
        refs[5 + i][...] = refs[i][...]


def on_device(
    d_out, saved_input, routes, probs, gate_pre, up_pre, gate_weight, up_weight, down_weight
):
    any_space = pl.BlockSpec(memory_space=pl.ANY)
    vmem = pl.BlockSpec(memory_space=pltpu.VMEM)
    dma = pltpu.SemaphoreType.DMA
    weight_grad = jax.ShapeDtypeStruct((HS, D), F32)
    shapes = (
        jax.ShapeDtypeStruct((T, D), BF16),
        jax.ShapeDtypeStruct((TOP, T), BF16),
        weight_grad,
        weight_grad,
        weight_grad,
    )
    results = pl.pallas_call(
        body,
        out_shape=shapes,
        in_specs=[any_space] * 2 + [vmem] * 4 + [any_space] * 3,
        out_specs=(vmem, vmem, any_space, any_space, any_space),
        scratch_shapes=[
            pltpu.VMEM((3, NX, HS, D), BF16),
            pltpu.VMEM((2, NZ, T, D), BF16),
            pltpu.VMEM((NYS, NG, GR, CW), BF16),
            pltpu.VMEM((2, NG, GR, D), BF16),
            pltpu.VMEM((NG, GR, NZ * T), BF16),
            pltpu.VMEM((NZ * T, S), BF16),
            pltpu.VMEM((NX, HS, S), BF16),
            pltpu.VMEM((NX, HS, S), BF16),
            pltpu.VMEM((NX, HS, S), BF16),
            pltpu.VMEM((S, H), BF16),
            pltpu.VMEM((S, H), BF16),
            pltpu.VMEM((NX, HS, D), BF16),
            pltpu.VMEM((NX, HS, D), BF16),
            pltpu.VMEM((7, T, D), BF16),
            pltpu.VMEM((3, HS, D), BF16),
            pltpu.VMEM((3, 2, HS, D), BF16),
            pltpu.VMEM((HS, D), F32),
            pltpu.VMEM((8, S), F32),
        ]
        + [pltpu.VMEM((8, 16, T), BF16)] * 8
        + [dma((3, 4)), dma((3, 4)), dma((3, NK, 3)), dma((3, NK, 3))]
        + [dma((NT, 7)), dma((NT, 7)), dma((NB, 7)), dma((NB, 7))]
        + [dma((NT, 7)), dma((NT, 7)), dma((NB, 7)), dma((NB, 7))]
        + [dma((7,))] * 8
        + [dma((NT + 3,)), dma((3, NK))],
        compiler_params=pltpu.CompilerParams(
            collective_id=0, has_side_effects=True, vmem_limit_bytes=63 * 2**20
        ),
        cost_estimate=pl.CostEstimate(
            flops=16 * 10**9, bytes_accessed=20 * 10**6, transcendentals=10**6
        ),
    )(
        d_out, saved_input, routes.T, probs.T, gate_pre.T, up_pre.T,
        down_weight[0], gate_weight[0], up_weight[0],
    )
    half = D // 2
    whole = pl.BlockSpec((TOP, T), lambda i: (0, 0))
    token_part = pl.BlockSpec((T, half), lambda i: (0, i))
    weight_part = pl.BlockSpec((HS, half), lambda i: (0, i))
    blocks = (token_part, whole, weight_part, weight_part, weight_part)
    d_tokens, d_probs, down_grad, gate_grad, up_grad = pl.pallas_call(
        hand_out, grid=(2,), out_shape=shapes, in_specs=blocks, out_specs=blocks
    )(*results)
    return d_tokens, d_probs.T, gate_grad[None], up_grad[None], down_grad[None]


def solution(mesh):
    token = P(("rep", "ep"), None)
    weight = P("ep", "rep", None)
    return jax.shard_map(
        on_device,
        mesh=mesh,
        in_specs=(token,) * 6 + (weight,) * 3,
        out_specs=(token, token, weight, weight, weight),
        check_vma=False,
    )
```

```python
import jax
import jax.numpy as jnp
from jax import lax
from jax.experimental import pallas as pl
from jax.experimental.pallas import tpu as pltpu
from jax.sharding import PartitionSpec as P

NX, NY, NZ, NC = 4, 4, 8, 2
NG = NY * NC
CAP, TOP = 13, 6
T = 128
D, H = 2048, 704
HS = H // NX
NK = 4
CW = D // NK
THERE = [(0, 0, 512), (0, 512, 512), (0, 1024, 512), (0, 1536, 512)]
THERE += [(1, 0, 512), (1, 512, 512), (1, 1024, 512), (1, 1536, 512)]
BACK = [(0, 512), (512, 512), (1024, 512), (1536, 256), (1792, 256)]
NT, NB, NYS = len(THERE), len(BACK), 4
ORDER = [0, 1, 2, 3, 4, 5, NT, NT + 1, NT + 2, 6, NT + 3, 7, NT + 4]
TURN = {chunk: place for place, chunk in enumerate(ORDER)}
GR = 128
GS = 112
S = NG * GR
HALF = D // 2
DOWN, GATE, UP = 0, 1, 2
MESH = pl.DeviceIdType.MESH
F32, BF16 = jnp.float32, jnp.bfloat16
Y_OFFSETS = [(2, 0), (1, 0), (3, 0), (2, 1), (1, 1), (3, 1), (0, 1)]


def nn(a, b):
    return jnp.dot(a, b, preferred_element_type=F32)


def nt(a, b):
    return lax.dot_general(a, b, (((1,), (1,)), ((), ())), preferred_element_type=F32)


def iota(shape, dim):
    return lax.broadcasted_iota(jnp.int32, shape, dim)


def div13(r):
    return (r * 79) >> 10


def body(
    d_out, saved, routes_t, probs_t, gpre, upre, dw, gw, uw,
    dtok, dprob, dg, gg, ug,
    wfull, zb, ys, slots, oh, oht, gp, up, aw, gbt, ubt, pt0, pt2, zrecv, xrel, xfin, stage, psum,
    meta_out, meta_in, ws, wr, ps, pr, dps, dpr,
    ag_s, ag_r, rs_s, rs_r, zs_s, zs_r, tz_s, tz_r, yd_s, yd_r, yr_s, yr_r,
    m_s, m_r, w_s, w_r, p_s, p_r, q_s, q_r, loc, out_sem,
):
    x = lax.axis_index("rep")
    ep = lax.axis_index("ep")
    core = lax.rem(ep, NC)
    z = lax.rem(ep // NC, NZ)
    y = ep // (NC * NZ)
    me_g = y * NC + core

    def at_x(d):
        return lax.rem(x + d + NX, NX)

    def at_z(d):
        return lax.rem(z + d + NZ, NZ)

    def dev_x(d):
        return (at_x(d), ep)

    def dev_z(d):
        return (x, (y * NZ + at_z(d)) * NC + core)

    def dev_y(i):
        dy, dc = Y_OFFSETS[i]
        y2, c2 = lax.rem(y + dy, NY), lax.rem(core + dc, NC)
        return y2 * NC + c2, (x, (y2 * NZ + z) * NC + c2)

    def remote(src, dst, send, recv, device):
        return pltpu.make_async_remote_copy(
            src_ref=src, dst_ref=dst, send_sem=send, recv_sem=recv,
            device_id=device, device_id_type=MESH,
        )

    barrier = pltpu.get_barrier_semaphore()
    peers = [dev_x(1), dev_x(-1)] + [dev_z(d) for d in range(1, NZ)]
    peers += [dev_y(i)[1] for i in range(len(Y_OFFSETS))]
    for device in peers:
        pl.semaphore_signal(barrier, inc=1, device_id=device, device_id_type=MESH)

    own = []
    for n, (a, col, width) in enumerate(THERE):
        cols = pl.ds(col, width)
        ref = (d_out, saved)[a]
        own.append(pltpu.make_async_copy(ref.at[:, cols], zb.at[a, z, :, cols], loc.at[n]))
    for cp in own:
        cp.start()
    shards = (dw, gw, uw)
    own_w = [pltpu.make_async_copy(shards[a], wfull.at[a, x], loc.at[NT + a]) for a in range(3)]
    for cp in own_w:
        cp.start()
    pl.semaphore_wait(barrier, len(peers))

    def ag_copy(a, i):
        if i == 0:
            return remote(shards[a], wfull.at[a, x], ag_s.at[a, 0], ag_r.at[a, 0], dev_x(1))
        if i == 1:
            return remote(shards[a], wfull.at[a, x], ag_s.at[a, 1], ag_r.at[a, 1], dev_x(-1))
        if i == 2:
            ref = wfull.at[a, at_x(-1), :, pl.ds(0, HALF)]
            return remote(ref, ref, ag_s.at[a, 2], ag_r.at[a, 2], dev_x(1))
        ref = wfull.at[a, at_x(1), :, pl.ds(HALF, HALF)]
        return remote(ref, ref, ag_s.at[a, 3], ag_r.at[a, 3], dev_x(-1))

    def ag_start(a):
        ag_copy(a, 0).start()
        ag_copy(a, 1).start()

    def ag_relay(a):
        ag_copy(a, 0).wait_recv()
        ag_copy(a, 2).start()
        ag_copy(a, 1).wait_recv()
        ag_copy(a, 3).start()

    def ag_finish(a):
        ag_copy(a, 2).wait_recv()
        ag_copy(a, 3).wait_recv()
        own_w[a].wait()
        for i in range(4):
            ag_copy(a, i).wait_send()

    def hops(k):
        return (4, 3) if k % 2 == 0 else (3, 4)

    def zag_copy(n, way, s):
        a, col, width = THERE[n]
        sign = 1 if way == 0 else -1
        i = s if way == 0 else hops(n)[0] + s
        ref = zb.at[a, at_z(-sign * s), :, pl.ds(col, width)]
        return remote(ref, ref, zs_s.at[n, i], zs_r.at[n, i], dev_z(sign))

    def zag_step(n, s):
        if s == 0:
            own[n].wait()
        for way in range(2):
            if 1 <= s <= hops(n)[way]:
                zag_copy(n, way, s - 1).wait_recv()
            if s < hops(n)[way]:
                zag_copy(n, way, s).start()

    def yd_copy(n, i):
        a, col, width = THERE[n]
        g, device = dev_y(i)
        return remote(
            ys.at[TURN[n] % NYS, g, pl.ds(0, GS), pl.ds(0, width)],
            slots.at[a, me_g, pl.ds(0, GS), pl.ds(col, width)],
            yd_s.at[n, i], yd_r.at[n, i], device,
        )

    def sent(chunk):
        for i in range(7):
            (yd_copy(chunk, i) if chunk < NT else yr_copy(chunk - NT, i)).wait_send()

    def free_buffer(chunk):
        if TURN[chunk] >= NYS:
            sent(ORDER[TURN[chunk] - NYS])

    def dispatch(n):
        a, col, width = THERE[n]
        for way in range(2):
            for s in range(hops(n)[way]):
                zag_copy(n, way, s).wait_send()
        free_buffer(n)
        rows = nn(oh[...].reshape(S, NZ * T), zb[a, :, :, pl.ds(col, width)].reshape(NZ * T, width))
        ys[TURN[n] % NYS, :, :, pl.ds(0, width)] = rows.astype(BF16).reshape(NG, GR, width)
        for i in range(7):
            yd_copy(n, i).start()
        slots[a, me_g, :, pl.ds(col, width)] = ys[TURN[n] % NYS, me_g, :, pl.ds(0, width)]

    def arrived(n):
        for i in range(7):
            yd_copy(n, i).wait_recv()

    def m_copy(d):
        return remote(meta_out.at[at_z(d)], meta_in.at[z], m_s.at[d - 1], m_r.at[d - 1], dev_z(d))

    def w_copy(i):
        g, device = dev_y(i)
        return remote(ws.at[g], wr.at[me_g], w_s.at[i], w_r.at[i], device)

    def p_copy(i):
        g, device = dev_y(i)
        return remote(ps.at[g], pr.at[me_g], p_s.at[i], p_r.at[i], device)

    def q_copy(d):
        return remote(dps.at[at_z(d)], dpr.at[z], q_s.at[d - 1], q_r.at[d - 1], dev_z(d))

    def expert_of_row():
        q = iota((NZ * NG, T), 0)
        return (((q >> 1) & 3) * NZ + (q >> 3)) * NC + (q & 1)

    def send_meta():
        ids = expert_of_row()
        hit_sum = jnp.zeros((NZ * NG, T), F32)
        prob_sum = jnp.zeros((NZ * NG, T), F32)
        for k in range(TOP):
            hit = ids == routes_t[k : k + 1, :]
            hit_sum = hit_sum + jnp.where(hit, 1.0, 0.0)
            prob_sum = prob_sum + jnp.where(hit, probs_t[k : k + 1, :].astype(F32), 0.0)
        before = jnp.where(iota((T, T), 0) < iota((T, T), 1), 1.0, 0.0).astype(BF16)
        rank = hit_sum * (nn(hit_sum.astype(BF16), before) + 1.0)
        for d in range(NZ):
            part = slice(d * NG, (d + 1) * NG)
            meta_out[d] = jnp.concatenate([rank[part], prob_sum[part]], axis=0).astype(BF16)
        for d in range(1, NZ):
            m_copy(d).start()
        meta_in[z] = meta_out[z]

    def permute_slots():
        def some(cg, carry):
            n = cg * 256 + iota((1, 256), 1)
            g, r = n >> 7, n & 127
            zr = div13(r)
            slot = (((g >> 1) * NZ + zr) * NC + (g & 1)) * CAP + (r - zr * CAP)
            slot = jnp.where(r < NZ * CAP, slot, -1)
            perm = jnp.where(iota((NG * NZ * CAP, 256), 0) == slot, 1.0, 0.0).astype(BF16)
            cols = pl.ds(pl.multiple_of(cg * 256, 256), 256)
            for j in range(NX):
                gp[j, :, cols] = nn(gpre[pl.ds(j * HS, HS), :], perm).astype(BF16)
                up[j, :, cols] = nn(upre[pl.ds(j * HS, HS), :], perm).astype(BF16)
            return carry

        lax.fori_loop(0, S // 256, some, 0)

    def build_tables():
        for d in range(1, NZ):
            m_copy(d).wait()
        table = jnp.concatenate([meta_in[d].astype(F32) for d in range(NZ)], axis=1)
        r = iota((GR, NZ * T), 0)
        zr = div13(r)
        key = jnp.where(
            (zr == (iota((GR, NZ * T), 1) >> 7)) & (r < NZ * CAP), r - zr * CAP + 1, -1
        ).astype(F32)
        for g in range(NG):
            oh[g] = jnp.where(table[g : g + 1, :] == key, 1.0, 0.0).astype(BF16)
        table16 = table.astype(BF16)
        for g in range(NG):
            rows = nt(table16, oh[g])
            ws[g] = jnp.broadcast_to(rows[NG + g : NG + g + 1, :], (16, GR)).astype(BF16)
        for i in range(7):
            w_copy(i).start()
        wr[me_g] = ws[me_g]

    def transpose_tables():
        for g in range(NG):
            oht[:, pl.ds(g * GR, GR)] = oh[g].T

    def slot_weight():
        return jnp.concatenate([wr[g][0:1, :].astype(F32) for g in range(NG)], axis=1)

    def activation(j):
        gate_val, up_val = gp[j].astype(F32), up[j].astype(F32)
        logistic = 1.0 / (1.0 + jnp.exp(-gate_val))
        silu = gate_val * logistic
        return gate_val, up_val, logistic, silu, (silu * up_val).astype(BF16).astype(F32)

    def tile_act(j):
        aw[j] = (slot_weight() * activation(j)[4]).astype(BF16)

    def tile_back(j):
        back = jnp.zeros((HS, S), F32)
        for k in range(NK):
            cols = pl.ds(k * CW, CW)
            back = back + nt(wfull[DOWN, j, :, cols], slots[0, :, :, cols].reshape(S, CW))
        gate_val, up_val, logistic, silu, act = activation(j)
        total = jnp.sum(back * act, axis=0, keepdims=True)
        if j == 0:
            psum[0:1, :] = total
        else:
            psum[0:1, :] = psum[0:1, :] + total
        scaled = slot_weight() * back
        gp[j] = (scaled * up_val * logistic * (1.0 + gate_val * (1.0 - logistic))).astype(BF16)
        up[j] = (scaled * silu).astype(BF16)

    parts = (pt0, wfull.at[DOWN], pt2)
    lefts = (aw, gp, up)

    def rs_copy(a, k, i):
        p, cols = parts[a], pl.ds(k * CW, CW)
        sign = 1 if k % 2 == 0 else -1
        if i == 0:
            src, dst, device = p.at[at_x(2), :, cols], xrel.at[a, :, cols], dev_x(sign)
        elif i == 1:
            src, dst, device = p.at[at_x(-sign), :, cols], xfin.at[a, 1, :, cols], dev_x(-sign)
        else:
            src, dst, device = p.at[at_x(sign), :, cols], xfin.at[a, 0, :, cols], dev_x(sign)
        return remote(src, dst, rs_s.at[a, k, i], rs_r.at[a, k, i], device)

    def part(a, k):
        cols = pl.ds(k * CW, CW)
        for j in range(NX):
            rows = nn(lefts[a][j], slots[min(a, 1), :, :, cols].reshape(S, CW))
            parts[a][j, :, cols] = rows.astype(BF16)
        rs_copy(a, k, 0).start()
        rs_copy(a, k, 1).start()

    def rs_relay(a, k):
        p, cols = parts[a], pl.ds(k * CW, CW)
        to = at_x(1 if k % 2 == 0 else -1)
        rs_copy(a, k, 0).wait_recv()
        p[to, :, cols] = (p[to, :, cols].astype(F32) + xrel[a, :, cols].astype(F32)).astype(BF16)
        rs_copy(a, k, 2).start()

    def out_copy(a, k):
        cols = pl.ds(k * CW, CW)
        return pltpu.make_async_copy(
            stage.at[:, cols], (dg, gg, ug)[a].at[:, cols], out_sem.at[a, k]
        )

    def rs_finish(a, k):
        cols = pl.ds(k * CW, CW)
        rs_copy(a, k, 1).wait_recv()
        rs_copy(a, k, 2).wait_recv()
        if a != DOWN:
            out_copy(a - 1, k).wait()
        total = xfin[a, 0, :, cols].astype(F32) + xfin[a, 1, :, cols].astype(F32)
        stage[:, cols] = parts[a][x, :, cols].astype(F32) + total
        out_copy(a, k).start()
        for i in range(3):
            rs_copy(a, k, i).wait_send()

    def yr_copy(k, i):
        col, width = BACK[k]
        g, device = dev_y(i)
        return remote(
            ys.at[TURN[NT + k] % NYS, g, pl.ds(0, GS), pl.ds(0, width)],
            zb.at[0, me_g, pl.ds(0, GS), pl.ds(col, width)],
            yr_s.at[k, i], yr_r.at[k, i], device,
        )

    def give_back(k):
        col, width = BACK[k]
        cols, slot = pl.ds(col, width), TURN[NT + k] % NYS
        free_buffer(NT + k)
        rows = nn(gbt[...], wfull[GATE, :, :, cols].reshape(H, width))
        rows = rows + nn(ubt[...], wfull[UP, :, :, cols].reshape(H, width))
        ys[slot, :, :, pl.ds(0, width)] = rows.astype(BF16).reshape(NG, GR, width)
        for i in range(7):
            yr_copy(k, i).start()
        zb[0, me_g, :, cols] = ys[slot, me_g, :, pl.ds(0, width)]

    def tz_copy(k, way, s):
        cols = pl.ds(*BACK[k])
        sign = 1 if way == 0 else -1
        count = hops(k)[way]
        i = s if way == 0 else hops(k)[0] + s
        return remote(
            zb.at[1, at_z(sign * (count - s)), :, cols], zrecv.at[i, :, cols],
            tz_s.at[k, i], tz_r.at[k, i], dev_z(sign),
        )

    def combine(k):
        col, width = BACK[k]
        cols = pl.ds(col, width)
        for i in range(7):
            yr_copy(k, i).wait_recv()
        total = nn(oht[...], zb[0, :, :, cols].reshape(S, width))
        zb[1, :, :, cols] = total.astype(BF16).reshape(NZ, T, width)

    def tz_step(k, s):
        cols = pl.ds(*BACK[k])
        if s == 0:
            combine(k)
        for way in range(2):
            sign, count = (1 if way == 0 else -1), hops(k)[way]
            base = 0 if way == 0 else hops(k)[0]
            if 1 <= s <= count:
                tz_copy(k, way, s - 1).wait_recv()
            if s < count:
                if s >= 1:
                    to = at_z(sign * (count - s))
                    zb[1, to, :, cols] = (
                        zb[1, to, :, cols].astype(F32) + zrecv[base + s - 1, :, cols].astype(F32)
                    ).astype(BF16)
                tz_copy(k, way, s).start()
        if s == 4:
            first, second = hops(k)
            total = zb[1, z, :, cols].astype(F32) + zrecv[first - 1, :, cols].astype(F32)
            total = total + zrecv[first + second - 1, :, cols].astype(F32)
            dtok[:, cols] = total.astype(BF16)

    def send_probs():
        for g in range(NG):
            ps[g] = jnp.broadcast_to(psum[0:1, pl.ds(g * GR, GR)], (16, GR)).astype(BF16)
        for i in range(7):
            p_copy(i).start()
        pr[me_g] = ps[me_g]

    def transpose_backs():
        for g in range(NG):
            cols = pl.ds(g * GR, GR)
            gbt[cols, :] = gp[:, :, cols].reshape(H, GR).T
            ubt[cols, :] = up[:, :, cols].reshape(H, GR).T

    def return_probs():
        for i in range(7):
            p_copy(i).wait()
        dense = jnp.concatenate([nn(pr[g], oh[g])[0:1, :] for g in range(NG)], axis=0)
        for d in range(NZ):
            some = dense[:, d * T : (d + 1) * T]
            dps[d] = jnp.concatenate([some, jnp.zeros((16 - NG, T), F32)], axis=0).astype(BF16)
        for d in range(1, NZ):
            q_copy(d).start()
        dpr[z] = dps[z]

    def pick_probs():
        for d in range(1, NZ):
            q_copy(d).wait()
        ids = expert_of_row()
        table = jnp.concatenate([dpr[d][0:NG, :].astype(F32) for d in range(NZ)], axis=0)
        rows = []
        for k in range(TOP):
            hit = ids == routes_t[k : k + 1, :]
            rows.append(jnp.sum(jnp.where(hit, table, 0.0), axis=0, keepdims=True))
        dprob[...] = jnp.concatenate(rows, axis=0).astype(BF16)

    zag_step(0, 0)
    send_meta()
    zag_step(1, 0)
    ag_start(0)
    ag_start(1)
    for a in range(2):
        slots[a, :, pl.ds(GS, GR - GS), :] = jnp.zeros((NG, GR - GS, D), BF16)

    for slot in range(1, NT + 4):
        for s in range(4, -1, -1):
            n = slot - s
            if 0 <= n < NT and (n, s) not in ((0, 0), (1, 0)):
                zag_step(n, s)
                if s == 4 and n < 6:
                    dispatch(n)
        if slot == 2:
            build_tables()
        if slot == 4:
            ag_relay(0)
            ag_start(2)
            ag_relay(1)
            permute_slots()
        if slot == 5:
            for i in range(7):
                w_copy(i).wait()
            for j in range(NX):
                tile_act(j)
        if slot == 6:
            ag_relay(2)
            arrived(0)
            part(DOWN, 0)
        if slot == 7:
            arrived(1)
            part(DOWN, 1)
            ag_finish(0)
        if slot == 8:
            arrived(2)
            part(DOWN, 2)
            transpose_tables()
        if slot == 9:
            arrived(3)
            part(DOWN, 3)
            tile_back(0)
            tile_back(1)
        if slot == 10:
            tile_back(2)
            tile_back(3)
            send_probs()
            transpose_backs()
            ag_finish(1)
            ag_finish(2)
            give_back(0)
            give_back(1)
            rs_relay(DOWN, 0)
    give_back(2)
    rs_relay(DOWN, 1)
    arrived(4)
    part(GATE, 0)
    part(UP, 0)
    rs_relay(DOWN, 2)
    dispatch(6)
    rs_relay(DOWN, 3)
    arrived(5)
    part(GATE, 1)
    part(UP, 1)
    return_probs()
    tz_step(0, 0)
    give_back(3)
    tz_step(0, 1)
    tz_step(1, 0)
    dispatch(7)
    rs_relay(GATE, 0)
    rs_relay(UP, 0)
    tz_step(0, 2)
    tz_step(1, 1)
    tz_step(2, 0)
    give_back(4)
    pick_probs()
    rs_relay(GATE, 1)
    rs_relay(UP, 1)
    tz_step(0, 3)
    tz_step(1, 2)
    tz_step(2, 1)
    arrived(6)
    part(GATE, 2)
    part(UP, 2)
    tz_step(0, 4)
    tz_step(1, 3)
    tz_step(2, 2)
    tz_step(3, 0)
    for k in range(NK):
        rs_finish(DOWN, k)
    tz_step(1, 4)
    tz_step(2, 3)
    tz_step(3, 1)
    rs_relay(GATE, 2)
    rs_relay(UP, 2)
    tz_step(2, 4)
    tz_step(3, 2)
    arrived(7)
    part(GATE, 3)
    part(UP, 3)
    tz_step(3, 3)
    tz_step(4, 0)
    for k in range(2):
        rs_finish(GATE, k)
        rs_finish(UP, k)
    tz_step(3, 4)
    tz_step(4, 1)
    rs_relay(GATE, 3)
    rs_relay(UP, 3)
    tz_step(4, 2)
    rs_finish(GATE, 2)
    rs_finish(UP, 2)
    tz_step(4, 3)
    tz_step(4, 4)
    rs_finish(GATE, 3)
    rs_finish(UP, 3)
    for k in range(NB):
        for way in range(2):
            for s in range(hops(k)[way]):
                tz_copy(k, way, s).wait_send()
    for chunk in ORDER[-NYS:]:
        sent(chunk)
    for k in range(NK):
        out_copy(UP, k).wait()


def hand_out(*refs):
    for i in range(5):
        refs[5 + i][...] = refs[i][...]


def on_device(
    d_out, saved_input, routes, probs, gate_pre, up_pre, gate_weight, up_weight, down_weight
):
    any_space = pl.BlockSpec(memory_space=pl.ANY)
    vmem = pl.BlockSpec(memory_space=pltpu.VMEM)
    dma = pltpu.SemaphoreType.DMA
    weight_grad = jax.ShapeDtypeStruct((HS, D), F32)
    shapes = (
        jax.ShapeDtypeStruct((T, D), BF16),
        jax.ShapeDtypeStruct((TOP, T), BF16),
        weight_grad,
        weight_grad,
        weight_grad,
    )
    results = pl.pallas_call(
        body,
        out_shape=shapes,
        in_specs=[any_space] * 2 + [vmem] * 4 + [any_space] * 3,
        out_specs=(vmem, vmem, any_space, any_space, any_space),
        scratch_shapes=[
            pltpu.VMEM((3, NX, HS, D), BF16),
            pltpu.VMEM((2, NZ, T, D), BF16),
            pltpu.VMEM((NYS, NG, GR, CW), BF16),
            pltpu.VMEM((2, NG, GR, D), BF16),
            pltpu.VMEM((NG, GR, NZ * T), BF16),
            pltpu.VMEM((NZ * T, S), BF16),
            pltpu.VMEM((NX, HS, S), BF16),
            pltpu.VMEM((NX, HS, S), BF16),
            pltpu.VMEM((NX, HS, S), BF16),
            pltpu.VMEM((S, H), BF16),
            pltpu.VMEM((S, H), BF16),
            pltpu.VMEM((NX, HS, D), BF16),
            pltpu.VMEM((NX, HS, D), BF16),
            pltpu.VMEM((7, T, D), BF16),
            pltpu.VMEM((3, HS, D), BF16),
            pltpu.VMEM((3, 2, HS, D), BF16),
            pltpu.VMEM((HS, D), F32),
            pltpu.VMEM((8, S), F32),
        ]
        + [pltpu.VMEM((8, 16, T), BF16)] * 8
        + [dma((3, 4)), dma((3, 4)), dma((3, NK, 3)), dma((3, NK, 3))]
        + [dma((NT, 7)), dma((NT, 7)), dma((NB, 7)), dma((NB, 7))]
        + [dma((NT, 7)), dma((NT, 7)), dma((NB, 7)), dma((NB, 7))]
        + [dma((7,))] * 8
        + [dma((NT + 3,)), dma((3, NK))],
        compiler_params=pltpu.CompilerParams(
            collective_id=0, has_side_effects=True, vmem_limit_bytes=63 * 2**20
        ),
        cost_estimate=pl.CostEstimate(
            flops=16 * 10**9, bytes_accessed=20 * 10**6, transcendentals=10**6
        ),
    )(
        d_out, saved_input, routes.T, probs.T, gate_pre.T, up_pre.T,
        down_weight[0], gate_weight[0], up_weight[0],
    )
    half = D // 2
    whole = pl.BlockSpec((TOP, T), lambda i: (0, 0))
    token_part = pl.BlockSpec((T, half), lambda i: (0, i))
    weight_part = pl.BlockSpec((HS, half), lambda i: (0, i))
    blocks = (token_part, whole, weight_part, weight_part, weight_part)
    d_tokens, d_probs, down_grad, gate_grad, up_grad = pl.pallas_call(
        hand_out, grid=(2,), out_shape=shapes, in_specs=blocks, out_specs=blocks
    )(*results)
    return d_tokens, d_probs.T, gate_grad[None], up_grad[None], down_grad[None]


def solution(mesh):
    token = P(("rep", "ep"), None)
    weight = P("ep", "rep", None)
    return jax.shard_map(
        on_device,
        mesh=mesh,
        in_specs=(token,) * 6 + (weight,) * 3,
        out_specs=(token, token, weight, weight, weight),
        check_vma=False,
    )
```
